32 devices in a mesh: dp: 16 (over z, x, core), tensor: 2 (over y).
Axes of the slice: x: 2, y: 2, z: 4, core: 2. Of those that a mesh axis runs over, the one named last changes fastest.
Arguments:
- acts: bfloat16 [2048, 2048], P('dp', 'tensor'), may hold values from -54 to 54
- partner: bfloat16 [2048, 2048], P('dp', 'tensor'), may hold values from -54 to 54
- hidden: bfloat16 [14336, 2048], P('dp', 'tensor'), may hold values from -6 to 6
- down_weight: bfloat16 [14336, 2048], P('dp', 'tensor'), may hold values from -0.046875 to 0.046875
Outputs:
- grad_hidden: bfloat16 [14336, 2048], P('dp', 'tensor')
- grad_weight: float32 [14336, 2048], P('dp', 'tensor')
- cka: float32 [], replicated
The draws below stay inside these ranges and needn't reach their ends.
All inputs are finite; a program needn't handle non-finite values.
Results may differ from the reference program's by a relative error of at most 0.0059.
Values may be sent and summed in bfloat16 or wider, within the bound.
A program may use at most 64 MiB of HBM per device.

```python
import jax
import jax.numpy as jnp
from jax import lax

D = 2048
DY = 2048
FF = 14336
TOK = 128
TOKENS = 2048
LOSS_SCALE = 4194304
N_DP = 16


def feature_draw(key, rows, cols):
    key_row, key_col, key_mean, key_base = jax.random.split(key, 4)
    place = jnp.arange(rows, dtype=jnp.float32) / rows
    base = jnp.clip(jax.random.normal(key_base, (rows, cols), jnp.float32), -3.5, 3.5)
    trend = 0.8 + 0.6 * place
    row_scale = trend[:, None] * jnp.exp(jax.random.uniform(key_row, (rows, 1), jnp.float32, -1.15, 1.15))
    col_scale = jnp.exp(jax.random.uniform(key_col, (1, cols), jnp.float32, -1.15, 1.15))
    col_mean = 0.5 * jnp.clip(jax.random.normal(key_mean, (1, cols), jnp.float32), -3.0, 3.0)
    return (base * row_scale + col_mean) * col_scale


def draw_acts(key, part):
    return feature_draw(jax.random.fold_in(key, 11), TOKENS, D).astype(jnp.bfloat16)


def draw_partner(key, part):
    return feature_draw(jax.random.fold_in(key, 23), TOKENS, DY).astype(jnp.bfloat16)


def block_levels(stream_key, extent, cuts, low, largest):
    loudness, own = 1.0, jax.random.fold_in(stream_key, 6)
    for dim, parts in cuts:
        steps = jnp.exp(jax.random.uniform(jax.random.fold_in(own, dim), (parts,), jnp.float32, low / len(cuts), largest / len(cuts)))
        loudness = loudness * jnp.repeat(steps, extent[dim] // parts).reshape([-1 if axis == dim else 1 for axis in range(len(extent))])
    return loudness


def scatter_about(rng, dims, deviation, bound, pieces=(), kind=jnp.bfloat16):
    gain = block_levels(rng, dims, pieces, -0.22, 0.18) if pieces else 1.0
    entries = jax.random.normal(rng, dims, jnp.float32) * deviation * gain
    return jnp.minimum(jnp.maximum(entries, -bound), bound).astype(kind)


def setup_inputs(seed: int = 0) -> dict:
    seeds = jax.random.split(jax.random.key(seed), 5)
    return {
        "acts": draw_acts(jax.random.fold_in(seeds[4], 71), 0),
        "partner": draw_partner(jax.random.fold_in(seeds[4], 71), 0),
        "hidden": scatter_about(seeds[2], (FF, TOKENS), 1.0, 6.0, ((0, 16), (1, 2))),
        "down_weight": scatter_about(seeds[3], (FF, D), FF ** -0.5, 0.046875, ((0, 16), (1, 2))),
    }


def center(values, width):
    blocks = values.astype(jnp.float32).reshape(N_DP, TOK, width)
    return (blocks - lax.optimization_barrier(jnp.mean(blocks, axis=1, keepdims=True))).astype(jnp.bfloat16)

def reference(acts, partner, hidden, down_weight):
    xc = center(acts, D)
    yc = center(partner, DY)
    xf = xc.astype(jnp.float32)
    yf = yc.astype(jnp.float32)
    gram_x = jnp.einsum('bnd,bmd->bnm', xf, xf)
    gram_y = jnp.einsum('bnd,bmd->bnm', yf, yf)
    sxx = jnp.sum(gram_x * gram_x)
    syy = jnp.sum(gram_y * gram_y)
    sxy = jnp.sum(gram_x * gram_y)
    root = jnp.sqrt(sxx * syy)
    cka = sxy / root
    ratio = sxy / sxx
    coef = -2.0 * jnp.float32(LOSS_SCALE) / root
    mixed = gram_y - ratio * gram_x
    grad = coef * jnp.einsum('bnm,bmd->bnd', mixed, xf, precision=lax.Precision.HIGHEST)
    grad = grad.astype(jnp.bfloat16).reshape(TOKENS, D)
    grad_hidden = jnp.dot(down_weight, grad.T, preferred_element_type=jnp.float32).astype(jnp.bfloat16)
    grad_weight = jnp.dot(hidden, grad, preferred_element_type=jnp.float32)
    return (grad_hidden, grad_weight, cka)
```

```python
import functools

import jax
import jax.numpy as jnp
from jax import lax
from jax.experimental import pallas as pl
from jax.experimental.pallas import tpu as pltpu
from jax.sharding import PartitionSpec as P

MESH = pl.DeviceIdType.MESH
HIDDEN_PIECES = 7


def center_rows(values):
    floats = values.astype(jnp.float32)
    return (floats - jnp.mean(floats, axis=0, keepdims=True)).astype(jnp.bfloat16)


def token_gram(values):
    return lax.dot_general(
        values, values, (((1,), (1,)), ((), ())), preferred_element_type=jnp.float32
    )


def gather_kernel(
    n_dp, scale, acts_ref, partner_ref, hidden_ref, cols_ref, other_hidden_ref, cka_ref,
    grams, stats, mine,
    hid_send, hid_recv, gram_send, gram_recv, stat_send, stat_recv,
    up_send, up_recv, down_send, down_recv, sib_send, sib_recv, own_sem,
):
    tokens = acts_ref.shape[0]
    chips, blocks_half = n_dp // 2, n_dp // 2
    side = chips // 2
    dp, tensor = lax.axis_index("dp"), lax.axis_index("tensor")
    chip, core = dp // 2, dp % 2
    column = chip % 2
    pos = (1 - column) * (chip // 2) + column * (chips - 1 - chip // 2)

    def chip_at(place):
        far = place // side
        return (1 - far) * (2 * place) + far * (2 * (chips - 1 - place) + 1)

    def device_at(offset):
        return chip_at((pos + offset + chips) % chips) * 2 + core

    def rows_of(block):
        half = (block // blocks_half + tensor) % 2
        return (half * blocks_half + block % blocks_half) * tokens

    peer = (dp, 1 - tensor)
    sibling = (dp + 1 - 2 * core, tensor)
    above, below = (device_at(1), tensor), (device_at(-1), tensor)
    rounds = []
    bit = 1
    while bit < n_dp:
        rounds.append((dp + bit * (1 - 2 * ((dp // bit) % 2)), tensor))
        bit *= 2

    barrier = pltpu.get_barrier_semaphore()
    partners = [peer, above, below] + rounds
    for other in partners:
        pl.semaphore_signal(barrier, inc=1, device_id=other, device_id_type=MESH)
    pl.semaphore_wait(barrier, len(partners))

    piece = hidden_ref.shape[0] // HIDDEN_PIECES

    def send_hidden(i):
        rows = pl.ds(i * piece, piece)
        return pltpu.make_async_remote_copy(
            src_ref=hidden_ref.at[rows], dst_ref=other_hidden_ref.at[rows],
            send_sem=hid_send.at[i], recv_sem=hid_recv.at[i],
            device_id=peer, device_id_type=MESH,
        )

    hidden_copies = [send_hidden(i) for i in range(HIDDEN_PIECES)]
    hidden_copies[0].start()

    centered_x = center_rows(acts_ref[...])
    centered_y = center_rows(partner_ref[...])
    grams[0, 0] = token_gram(centered_x)
    grams[0, 1] = token_gram(centered_y)
    gram_copy = pltpu.make_async_remote_copy(
        src_ref=grams.at[0], dst_ref=grams.at[1], send_sem=gram_send, recv_sem=gram_recv,
        device_id=peer, device_id_type=MESH,
    )
    gram_copy.start()
    for copy in hidden_copies[1:]:
        copy.start()
    gram_copy.wait()
    gram_x = grams[0, 0] + grams[1, 0]
    gram_y = grams[0, 1] + grams[1, 1]

    stats[0] = jnp.zeros_like(stats[0])
    stats[0, 0:1] = jnp.sum(gram_x * gram_x, axis=0, keepdims=True)
    stats[0, 1:2] = jnp.sum(gram_y * gram_y, axis=0, keepdims=True)
    stats[0, 2:3] = jnp.sum(gram_x * gram_y, axis=0, keepdims=True)
    for i, other in enumerate(rounds):
        copy = pltpu.make_async_remote_copy(
            src_ref=stats.at[2 * i], dst_ref=stats.at[2 * i + 1],
            send_sem=stat_send.at[i], recv_sem=stat_recv.at[i],
            device_id=other, device_id_type=MESH,
        )
        copy.start()
        copy.wait()
        stats[2 * i + 2] = stats[2 * i] + stats[2 * i + 1]
    sums = jnp.sum(stats[2 * len(rounds)], axis=1, keepdims=True)
    sxx, syy, sxy = sums[0:1], sums[1:2], sums[2:3]
    root = jnp.sqrt(sxx * syy)
    cka_ref[...] = jnp.broadcast_to(sxy / root, cka_ref.shape)
    ratio = sxy / sxx
    coef = -2.0 * scale / root
    mixed = gram_y - ratio * gram_x
    grad = jnp.zeros(mine.shape, jnp.float32)
    rest = mixed
    for _ in range(3):
        top = rest.astype(jnp.bfloat16)
        rest = rest - top.astype(jnp.float32)
        grad += jnp.dot(top, centered_x, preferred_element_type=jnp.float32)
    mine[...] = (coef * grad).astype(jnp.bfloat16)

    own_rows = pl.ds(pl.multiple_of(rows_of(dp), tokens), tokens)
    own_copy = pltpu.make_async_copy(mine, cols_ref.at[own_rows], own_sem)
    own_copy.start()

    last = chips // 2

    def ring(step, way):
        block = device_at(-way * (step - 1))
        start, size = rows_of(block), tokens
        if step == last:
            size = tokens // 2
            start = start + (0 if way > 0 else size)
        rows = pl.ds(pl.multiple_of(start, size), size)
        sends, recvs = (up_send, up_recv) if way > 0 else (down_send, down_recv)
        return pltpu.make_async_remote_copy(
            src_ref=mine if step == 1 else cols_ref.at[rows], dst_ref=cols_ref.at[rows],
            send_sem=sends.at[step - 1], recv_sem=recvs.at[step - 1],
            device_id=above if way > 0 else below, device_id_type=MESH,
        )

    def share(i, block):
        rows = pl.ds(pl.multiple_of(rows_of(block), tokens), tokens)
        return pltpu.make_async_remote_copy(
            src_ref=mine if i == 0 else cols_ref.at[rows], dst_ref=cols_ref.at[rows],
            send_sem=sib_send.at[i], recv_sem=sib_recv.at[i],
            device_id=sibling, device_id_type=MESH,
        )

    ups = [ring(step, 1) for step in range(1, last + 1)]
    downs = [ring(step, -1) for step in range(1, last + 1)]
    ups[0].start()
    downs[0].start()
    shares = [share(0, dp)]
    shares[0].start()
    for step in range(1, last):
        for way, copies in ((1, ups), (-1, downs)):
            copies[step - 1].wait_recv()
            copies[step].start()
            shares.append(share(len(shares), device_at(-way * step)))
            shares[-1].start()
    ups[-1].wait_recv()
    downs[-1].wait_recv()
    shares.append(share(len(shares), device_at(last)))
    shares[-1].start()

    own_copy.wait()
    for copy in ups + downs:
        copy.wait_send()
    for copy in shares:
        copy.wait()
    for copy in hidden_copies:
        copy.wait()


def gather(acts, partner, hidden, scale):
    n_dp = lax.axis_size("dp")
    tokens, width = acts.shape
    rounds = n_dp.bit_length() - 1
    steps = n_dp // 4
    dma = pltpu.SemaphoreType.DMA
    vmem, anywhere = pl.BlockSpec(memory_space=pltpu.VMEM), pl.BlockSpec(memory_space=pl.ANY)
    return pl.pallas_call(
        functools.partial(gather_kernel, n_dp, scale),
        out_shape=(
            jax.ShapeDtypeStruct((n_dp * tokens, width), jnp.bfloat16),
            jax.ShapeDtypeStruct(hidden.shape, jnp.bfloat16),
            jax.ShapeDtypeStruct((8, 128), jnp.float32),
        ),
        in_specs=[vmem, vmem, anywhere],
        out_specs=(anywhere, anywhere, vmem),
        scratch_shapes=[
            pltpu.VMEM((2, 2, tokens, tokens), jnp.float32),
            pltpu.VMEM((2 * rounds + 1, 8, tokens), jnp.float32),
            pltpu.VMEM((tokens, width), jnp.bfloat16),
            dma((HIDDEN_PIECES,)), dma((HIDDEN_PIECES,)), dma, dma,
            dma((rounds,)), dma((rounds,)),
            dma((steps,)), dma((steps,)), dma((steps,)), dma((steps,)),
            dma((2 * steps,)), dma((2 * steps,)), dma,
        ],
        compiler_params=pltpu.CompilerParams(
            collective_id=0, has_side_effects=True, vmem_limit_bytes=32 * 2**20
        ),
    )(acts, partner, hidden)


def paired(acts, partner, hidden, down_weight):
    tokens = acts.shape[0]
    width = acts.shape[1] * lax.axis_size("tensor")
    scale = float(tokens * lax.axis_size("dp") * width)
    cols, other_hidden, cka = gather(acts, partner, hidden, scale)
    half = cols.shape[0] // 2
    own, other = cols[:half], cols[half:]
    contract = (((1,), (1,)), ((), ()))
    theirs = lax.dot_general(
        down_weight, other, contract, preferred_element_type=jnp.float32
    ).astype(jnp.bfloat16)
    arrived = lax.ppermute(theirs, "tensor", [(0, 1), (1, 0)])
    ours = lax.dot_general(down_weight, own, contract, preferred_element_type=jnp.float32)
    grad_weight = jnp.dot(hidden, own, preferred_element_type=jnp.float32) + jnp.dot(
        other_hidden, other, preferred_element_type=jnp.float32
    )
    ours, grad_weight, arrived = lax.optimization_barrier((ours, grad_weight, arrived))
    grad_hidden = (ours + arrived.astype(jnp.float32)).astype(jnp.bfloat16)
    return (grad_hidden, grad_weight, cka[0, 0])


def gathered(acts, partner, hidden, down_weight):
    rows = acts.shape[0]
    width = acts.shape[1] * lax.axis_size("tensor")
    total = rows * lax.axis_size("dp")
    scale = float(total * width)
    centered_x = center_rows(acts)
    centered_y = center_rows(partner)
    whole_x, whole_y = (
        lax.all_gather(centered_x, "tensor", axis=1, tiled=True),
        lax.all_gather(centered_y, "tensor", axis=1, tiled=True),
    )
    gram_x = token_gram(whole_x)
    gram_y = token_gram(whole_y)
    sxx, syy, sxy = lax.psum(
        (jnp.sum(gram_x * gram_x), jnp.sum(gram_y * gram_y), jnp.sum(gram_x * gram_y)), "dp"
    )
    root = jnp.sqrt(sxx * syy)
    cka = sxy / root
    ratio = sxy / sxx
    coef = -2.0 * scale / root
    mixed = gram_y - ratio * gram_x
    grad = (
        coef * jnp.dot(mixed, centered_x.astype(jnp.float32), precision=lax.Precision.HIGHEST)
    ).astype(jnp.bfloat16)
    columns = lax.all_gather(grad, "dp", axis=0, tiled=True)
    token_block = lax.all_to_all(columns, "tensor", split_axis=0, concat_axis=1, tiled=True)
    grad_hidden = lax.dot_general(
        lax.all_gather(down_weight, "tensor", axis=1, tiled=True),
        token_block,
        (((1,), (1,)), ((), ())),
        preferred_element_type=jnp.float32,
    ).astype(jnp.bfloat16)
    grad_weight = lax.dot_general(
        lax.all_gather(hidden, "tensor", axis=1, tiled=True),
        columns,
        (((1,), (0,)), ((), ())),
        preferred_element_type=jnp.float32,
    )
    return (grad_hidden, grad_weight, cka)


def solution(mesh):
    n_dp, n_tensor = mesh.shape["dp"], mesh.shape["tensor"]
    fits = n_tensor == 2 and n_dp >= 8 and n_dp & (n_dp - 1) == 0
    spec = P("dp", "tensor")
    return jax.shard_map(
        paired if fits else gathered,
        mesh=mesh, in_specs=(spec,) * 4, out_specs=(spec, spec, P()), check_vma=False,
    )
```

```python
import functools

import jax
import jax.numpy as jnp
from jax import lax
from jax.experimental import pallas as pl
from jax.experimental.pallas import tpu as pltpu
from jax.sharding import PartitionSpec as P

MESH = pl.DeviceIdType.MESH
TILE = 256


def center_rows(values):
    floats = values.astype(jnp.float32)
    return (floats - jnp.mean(floats, axis=0, keepdims=True)).astype(jnp.bfloat16)


def token_gram(values):
    return lax.dot_general(
        values, values, (((1,), (1,)), ((), ())), preferred_element_type=jnp.float32
    )


def gather_kernel(
    n_dp, scale, acts_ref, partner_ref, cols_ref, cka_ref,
    grams, stats, mine,
    gram_send, gram_recv, stat_send, stat_recv,
    up_send, up_recv, down_send, down_recv, sib_send, sib_recv, own_sem,
):
    tokens = acts_ref.shape[0]
    chips, blocks_half = n_dp // 2, n_dp // 2
    side = chips // 2
    dp, tensor = lax.axis_index("dp"), lax.axis_index("tensor")
    chip, core = dp // 2, dp % 2
    column = chip % 2
    pos = (1 - column) * (chip // 2) + column * (chips - 1 - chip // 2)

    def chip_at(place):
        far = place // side
        return (1 - far) * (2 * place) + far * (2 * (chips - 1 - place) + 1)

    def device_at(offset):
        return chip_at((pos + offset + chips) % chips) * 2 + core

    def rows_of(block):
        half = (block // blocks_half + tensor) % 2
        return (half * blocks_half + block % blocks_half) * tokens

    peer = (dp, 1 - tensor)
    sibling = (dp + 1 - 2 * core, tensor)
    above, below = (device_at(1), tensor), (device_at(-1), tensor)
    rounds = []
    bit = 1
    while bit < n_dp:
        rounds.append((dp + bit * (1 - 2 * ((dp // bit) % 2)), tensor))
        bit *= 2

    barrier = pltpu.get_barrier_semaphore()
    partners = [peer, above, below] + rounds
    for other in partners:
        pl.semaphore_signal(barrier, inc=1, device_id=other, device_id_type=MESH)
    pl.semaphore_wait(barrier, len(partners))

    centered_x = center_rows(acts_ref[...])
    centered_y = center_rows(partner_ref[...])
    grams[0, 0] = token_gram(centered_x)
    grams[0, 1] = token_gram(centered_y)
    gram_copy = pltpu.make_async_remote_copy(
        src_ref=grams.at[0], dst_ref=grams.at[1], send_sem=gram_send, recv_sem=gram_recv,
        device_id=peer, device_id_type=MESH,
    )
    gram_copy.start()
    gram_copy.wait()
    gram_x = grams[0, 0] + grams[1, 0]
    gram_y = grams[0, 1] + grams[1, 1]

    stats[0] = jnp.zeros_like(stats[0])
    stats[0, 0:1] = jnp.sum(gram_x * gram_x, axis=0, keepdims=True)
    stats[0, 1:2] = jnp.sum(gram_y * gram_y, axis=0, keepdims=True)
    stats[0, 2:3] = jnp.sum(gram_x * gram_y, axis=0, keepdims=True)
    for i, other in enumerate(rounds):
        copy = pltpu.make_async_remote_copy(
            src_ref=stats.at[2 * i], dst_ref=stats.at[2 * i + 1],
            send_sem=stat_send.at[i], recv_sem=stat_recv.at[i],
            device_id=other, device_id_type=MESH,
        )
        copy.start()
        copy.wait()
        stats[2 * i + 2] = stats[2 * i] + stats[2 * i + 1]
    sums = jnp.sum(stats[2 * len(rounds)], axis=1, keepdims=True)
    sxx, syy, sxy = sums[0:1], sums[1:2], sums[2:3]
    root = jnp.sqrt(sxx * syy)
    cka_ref[...] = jnp.broadcast_to(sxy / root, cka_ref.shape)
    ratio = sxy / sxx
    coef = -2.0 * scale / root
    mixed = gram_y - ratio * gram_x
    grad = jnp.zeros(mine.shape, jnp.float32)
    rest = mixed
    for _ in range(3):
        top = rest.astype(jnp.bfloat16)
        rest = rest - top.astype(jnp.float32)
        grad += jnp.dot(top, centered_x, preferred_element_type=jnp.float32)
    mine[...] = (coef * grad).astype(jnp.bfloat16)

    own_rows = pl.ds(pl.multiple_of(rows_of(dp), tokens), tokens)
    own_copy = pltpu.make_async_copy(mine, cols_ref.at[own_rows], own_sem)
    own_copy.start()

    last = chips // 2

    def ring(step, way):
        block = device_at(-way * (step - 1))
        start, size = rows_of(block), tokens
        if step == last:
            size = tokens // 2
            start = start + (0 if way > 0 else size)
        rows = pl.ds(pl.multiple_of(start, size), size)
        sends, recvs = (up_send, up_recv) if way > 0 else (down_send, down_recv)
        return pltpu.make_async_remote_copy(
            src_ref=mine if step == 1 else cols_ref.at[rows], dst_ref=cols_ref.at[rows],
            send_sem=sends.at[step - 1], recv_sem=recvs.at[step - 1],
            device_id=above if way > 0 else below, device_id_type=MESH,
        )

    def share(i, block):
        rows = pl.ds(pl.multiple_of(rows_of(block), tokens), tokens)
        return pltpu.make_async_remote_copy(
            src_ref=mine if i == 0 else cols_ref.at[rows], dst_ref=cols_ref.at[rows],
            send_sem=sib_send.at[i], recv_sem=sib_recv.at[i],
            device_id=sibling, device_id_type=MESH,
        )

    ups = [ring(step, 1) for step in range(1, last + 1)]
    downs = [ring(step, -1) for step in range(1, last + 1)]
    ups[0].start()
    downs[0].start()
    shares = [share(0, dp)]
    shares[0].start()
    for step in range(1, last):
        for way, copies in ((1, ups), (-1, downs)):
            copies[step - 1].wait_recv()
            copies[step].start()
            shares.append(share(len(shares), device_at(-way * step)))
            shares[-1].start()
    ups[-1].wait_recv()
    downs[-1].wait_recv()
    shares.append(share(len(shares), device_at(last)))
    shares[-1].start()

    own_copy.wait()
    for copy in ups + downs:
        copy.wait_send()
    for copy in shares:
        copy.wait()


def gather(acts, partner, scale):
    n_dp = lax.axis_size("dp")
    tokens, width = acts.shape
    rounds = n_dp.bit_length() - 1
    steps = n_dp // 4
    dma = pltpu.SemaphoreType.DMA
    vmem, anywhere = pl.BlockSpec(memory_space=pltpu.VMEM), pl.BlockSpec(memory_space=pl.ANY)
    return pl.pallas_call(
        functools.partial(gather_kernel, n_dp, scale),
        out_shape=(
            jax.ShapeDtypeStruct((n_dp * tokens, width), jnp.bfloat16),
            jax.ShapeDtypeStruct((8, 128), jnp.float32),
        ),
        in_specs=[vmem, vmem],
        out_specs=(anywhere, vmem),
        scratch_shapes=[
            pltpu.VMEM((2, 2, tokens, tokens), jnp.float32),
            pltpu.VMEM((2 * rounds + 1, 8, tokens), jnp.float32),
            pltpu.VMEM((tokens, width), jnp.bfloat16),
            dma, dma,
            dma((rounds,)), dma((rounds,)),
            dma((steps,)), dma((steps,)), dma((steps,)), dma((steps,)),
            dma((2 * steps,)), dma((2 * steps,)), dma,
        ],
        compiler_params=pltpu.CompilerParams(
            collective_id=0, has_side_effects=True, vmem_limit_bytes=32 * 2**20
        ),
        cost_estimate=pl.CostEstimate(
            flops=8 * tokens * tokens * width, transcendentals=0,
            bytes_accessed=80 * n_dp * tokens * width,
        ),
    )(acts, partner)


def by_tokens_kernel(weight_ref, grad_ref, out_ref):
    out_ref[...] = lax.dot_general(
        weight_ref[...], grad_ref[...], (((1,), (1,)), ((), ())), preferred_element_type=jnp.float32
    ).astype(out_ref.dtype)


def by_tokens(weight, cols, half, dtype):
    rows, width = weight.shape
    tokens = cols.shape[0] // 2
    tile = min(TILE, tokens)
    steps = tokens // tile
    return pl.pallas_call(
        by_tokens_kernel,
        grid=(steps,),
        out_shape=jax.ShapeDtypeStruct((rows, tokens), dtype),
        in_specs=[
            pl.BlockSpec((rows, width), lambda i: (0, 0)),
            pl.BlockSpec((tile, width), lambda i: (half * steps + i, 0)),
        ],
        out_specs=pl.BlockSpec((rows, tile), lambda i: (0, i)),
        compiler_params=pltpu.CompilerParams(vmem_limit_bytes=32 * 2**20),
        cost_estimate=pl.CostEstimate(
            flops=2 * rows * tokens * width, transcendentals=0,
            bytes_accessed=2 * (rows * width + tokens * width + 2 * rows * tokens),
        ),
    )(weight, cols)


def over_tokens_kernel(own_ref, other_ref, grad_own_ref, grad_other_ref, out_ref):
    out_ref[...] = jnp.dot(
        own_ref[...], grad_own_ref[...], preferred_element_type=jnp.float32
    ) + jnp.dot(other_ref[...], grad_other_ref[...], preferred_element_type=jnp.float32)


def over_tokens(own, other, cols):
    rows, tokens = own.shape
    width = cols.shape[1]
    tile = min(TILE, width)
    whole = pl.BlockSpec((rows, tokens), lambda i: (0, 0))
    return pl.pallas_call(
        over_tokens_kernel,
        grid=(width // tile,),
        out_shape=jax.ShapeDtypeStruct((rows, width), jnp.float32),
        in_specs=[
            whole, whole,
            pl.BlockSpec((tokens, tile), lambda i: (0, i)),
            pl.BlockSpec((tokens, tile), lambda i: (1, i)),
        ],
        out_specs=pl.BlockSpec((rows, tile), lambda i: (0, i)),
        compiler_params=pltpu.CompilerParams(vmem_limit_bytes=32 * 2**20),
        cost_estimate=pl.CostEstimate(
            flops=4 * rows * tokens * width, transcendentals=0,
            bytes_accessed=4 * (rows * tokens + tokens * width + rows * width),
        ),
    )(own, other, cols, cols)


def paired(acts, partner, hidden, down_weight):
    tokens = acts.shape[0]
    width = acts.shape[1] * lax.axis_size("tensor")
    scale = float(tokens * lax.axis_size("dp") * width)
    swap = [(0, 1), (1, 0)]
    other_hidden = lax.ppermute(hidden, "tensor", swap)
    cols, cka = gather(acts, partner, scale)
    theirs = by_tokens(down_weight, cols, 1, jnp.bfloat16)
    arrived = lax.ppermute(theirs, "tensor", swap)
    ours = by_tokens(down_weight, cols, 0, jnp.float32)
    grad_weight = over_tokens(hidden, other_hidden, cols)
    grad_hidden = (ours + arrived.astype(jnp.float32)).astype(jnp.bfloat16)
    return (grad_hidden, grad_weight, cka[0, 0])


def gathered(acts, partner, hidden, down_weight):
    rows = acts.shape[0]
    width = acts.shape[1] * lax.axis_size("tensor")
    total = rows * lax.axis_size("dp")
    scale = float(total * width)
    centered_x = center_rows(acts)
    centered_y = center_rows(partner)
    whole_x, whole_y = (
        lax.all_gather(centered_x, "tensor", axis=1, tiled=True),
        lax.all_gather(centered_y, "tensor", axis=1, tiled=True),
    )
    gram_x = token_gram(whole_x)
    gram_y = token_gram(whole_y)
    sxx, syy, sxy = lax.psum(
        (jnp.sum(gram_x * gram_x), jnp.sum(gram_y * gram_y), jnp.sum(gram_x * gram_y)), "dp"
    )
    root = jnp.sqrt(sxx * syy)
    cka = sxy / root
    ratio = sxy / sxx
    coef = -2.0 * scale / root
    mixed = gram_y - ratio * gram_x
    grad = (
        coef * jnp.dot(mixed, centered_x.astype(jnp.float32), precision=lax.Precision.HIGHEST)
    ).astype(jnp.bfloat16)
    columns = lax.all_gather(grad, "dp", axis=0, tiled=True)
    token_block = lax.all_to_all(columns, "tensor", split_axis=0, concat_axis=1, tiled=True)
    grad_hidden = lax.dot_general(
        lax.all_gather(down_weight, "tensor", axis=1, tiled=True),
        token_block,
        (((1,), (1,)), ((), ())),
        preferred_element_type=jnp.float32,
    ).astype(jnp.bfloat16)
    grad_weight = lax.dot_general(
        lax.all_gather(hidden, "tensor", axis=1, tiled=True),
        columns,
        (((1,), (0,)), ((), ())),
        preferred_element_type=jnp.float32,
    )
    return (grad_hidden, grad_weight, cka)


def solution(mesh):
    n_dp, n_tensor = mesh.shape["dp"], mesh.shape["tensor"]
    fits = n_tensor == 2 and n_dp >= 8 and n_dp & (n_dp - 1) == 0
    spec = P("dp", "tensor")
    return jax.shard_map(
        paired if fits else gathered,
        mesh=mesh, in_specs=(spec,) * 4, out_specs=(spec, spec, P()), check_vma=False,
    )
```

```python
import functools

import jax
import jax.numpy as jnp
from jax import lax
from jax.experimental import pallas as pl
from jax.experimental.pallas import tpu as pltpu
from jax.sharding import PartitionSpec as P

MESH = pl.DeviceIdType.MESH
FIRST = 64
PARTS = 4
TILE = 256


def center_rows(values):
    floats = values.astype(jnp.float32)
    return (floats - jnp.mean(floats, axis=0, keepdims=True)).astype(jnp.bfloat16)


def token_gram(values):
    return lax.dot_general(
        values, values, (((1,), (1,)), ((), ())), preferred_element_type=jnp.float32
    )


def fused_kernel(
    n_dp, scale, acts_hbm, partner_hbm, hidden_hbm, weight_hbm, grad_hidden_hbm, grad_weight_hbm, cka_ref,
    acts, partner, hidden, weight, other_hidden, cols, theirs, arrived, ours, grad_hidden, grad_weight, grams, stats,
    load_sem, weight_sem, store_sem, hid_send, hid_recv, gram_send, gram_recv, stat_send, stat_recv,
    up_send, up_recv, down_send, down_recv, sib_send, sib_recv, part_send, part_recv,
):
    tokens = acts.shape[0]
    rows = hidden.shape[0]
    chips, blocks_half = n_dp // 2, n_dp // 2
    side = chips // 2
    dp, tensor = lax.axis_index("dp"), lax.axis_index("tensor")
    chip, core = dp // 2, dp % 2
    column = chip % 2
    pos = (1 - column) * (chip // 2) + column * (chips - 1 - chip // 2)

    def chip_at(place):
        far = place // side
        return (1 - far) * (2 * place) + far * (2 * (chips - 1 - place) + 1)

    def device_at(offset):
        return chip_at((pos + offset + chips) % chips) * 2 + core

    def rows_of(block):
        half = (block // blocks_half + tensor) % 2
        return (half * blocks_half + block % blocks_half) * tokens

    loads = [
        pltpu.make_async_copy(source, target, load_sem.at[i])
        for i, (source, target) in enumerate(
            ((acts_hbm, acts), (partner_hbm, partner), (hidden_hbm, hidden), (weight_hbm, weight))
        )
    ]
    for load in loads:
        load.start()

    peer = (dp, 1 - tensor)
    sibling = (dp + 1 - 2 * core, tensor)
    above, below = (device_at(1), tensor), (device_at(-1), tensor)
    rounds = []
    bit = 1
    while bit < n_dp:
        rounds.append((dp + bit * (1 - 2 * ((dp // bit) % 2)), tensor))
        bit *= 2

    barrier = pltpu.get_barrier_semaphore()
    partners = [peer, above, below] + rounds
    for other in partners:
        pl.semaphore_signal(barrier, inc=1, device_id=other, device_id_type=MESH)
    pl.semaphore_wait(barrier, len(partners))

    def send_hidden(i, start, size):
        part = pl.ds(start, size)
        return pltpu.make_async_remote_copy(
            src_ref=hidden_hbm.at[part], dst_ref=other_hidden.at[part],
            send_sem=hid_send.at[i], recv_sem=hid_recv.at[i],
            device_id=peer, device_id_type=MESH,
        )

    hidden_copies = [send_hidden(0, 0, FIRST), send_hidden(1, FIRST, rows - FIRST)]
    hidden_copies[0].start()

    loads[0].wait()
    loads[1].wait()
    centered_x = center_rows(acts[...])
    centered_y = center_rows(partner[...])
    grams[0, 0] = token_gram(centered_x)
    grams[0, 1] = token_gram(centered_y)
    gram_copy = pltpu.make_async_remote_copy(
        src_ref=grams.at[0], dst_ref=grams.at[1], send_sem=gram_send, recv_sem=gram_recv,
        device_id=peer, device_id_type=MESH,
    )
    gram_copy.start()
    hidden_copies[1].start()
    gram_copy.wait()
    gram_x = grams[0, 0] + grams[1, 0]
    gram_y = grams[0, 1] + grams[1, 1]

    stats[0] = jnp.zeros_like(stats[0])
    stats[0, 0:1] = jnp.sum(gram_x * gram_x, axis=0, keepdims=True)
    stats[0, 1:2] = jnp.sum(gram_y * gram_y, axis=0, keepdims=True)
    stats[0, 2:3] = jnp.sum(gram_x * gram_y, axis=0, keepdims=True)
    for i, other in enumerate(rounds):
        copy = pltpu.make_async_remote_copy(
            src_ref=stats.at[2 * i], dst_ref=stats.at[2 * i + 1],
            send_sem=stat_send.at[i], recv_sem=stat_recv.at[i],
            device_id=other, device_id_type=MESH,
        )
        copy.start()
        copy.wait()
        stats[2 * i + 2] = stats[2 * i] + stats[2 * i + 1]
    sums = jnp.sum(stats[2 * len(rounds)], axis=1, keepdims=True)
    sxx, syy, sxy = sums[0:1], sums[1:2], sums[2:3]
    root = jnp.sqrt(sxx * syy)
    cka_ref[...] = jnp.broadcast_to(sxy / root, cka_ref.shape)
    ratio = sxy / sxx
    coef = -2.0 * scale / root
    mixed = gram_y - ratio * gram_x
    grad = jnp.zeros(centered_x.shape, jnp.float32)
    rest = mixed
    for _ in range(3):
        top = rest.astype(jnp.bfloat16)
        rest = rest - top.astype(jnp.float32)
        grad += jnp.dot(top, centered_x, preferred_element_type=jnp.float32)
    own_rows = pl.ds(pl.multiple_of(rows_of(dp), tokens), tokens)
    cols[own_rows] = (coef * grad).astype(jnp.bfloat16)

    last = chips // 2

    def ring(step, way):
        block = device_at(-way * (step - 1))
        start, size = rows_of(block), tokens
        if step == last:
            size = tokens // 2
            start = start + (0 if way > 0 else size)
        span = pl.ds(pl.multiple_of(start, size), size)
        sends, recvs = (up_send, up_recv) if way > 0 else (down_send, down_recv)
        return pltpu.make_async_remote_copy(
            src_ref=cols.at[span], dst_ref=cols.at[span],
            send_sem=sends.at[step - 1], recv_sem=recvs.at[step - 1],
            device_id=above if way > 0 else below, device_id_type=MESH,
        )

    def share(i, block):
        span = pl.ds(pl.multiple_of(rows_of(block), tokens), tokens)
        return pltpu.make_async_remote_copy(
            src_ref=cols.at[span], dst_ref=cols.at[span],
            send_sem=sib_send.at[i], recv_sem=sib_recv.at[i],
            device_id=sibling, device_id_type=MESH,
        )

    ups = [ring(step, 1) for step in range(1, last + 1)]
    downs = [ring(step, -1) for step in range(1, last + 1)]
    ups[0].start()
    downs[0].start()
    shares = [share(0, dp)]
    shares[0].start()
    for step in range(1, last):
        for way, copies in ((1, ups), (-1, downs)):
            copies[step - 1].wait_recv()
            copies[step].start()
            shares.append(share(len(shares), device_at(-way * step)))
            shares[-1].start()
    ups[-1].wait_recv()
    downs[-1].wait_recv()
    shares.append(share(len(shares), device_at(last)))
    shares[-1].start()

    for copy in ups + downs:
        copy.wait_send()
    for copy in shares:
        copy.wait()
    loads[2].wait()
    loads[3].wait()

    half = n_dp * tokens // 2
    size = rows // PARTS
    own, other = pl.ds(0, half), pl.ds(half, half)

    def span_of(i):
        return pl.ds(pl.multiple_of(i * size, 16), size)

    def send_part(i):
        span = span_of(i)
        return pltpu.make_async_remote_copy(
            src_ref=theirs.at[span], dst_ref=arrived.at[span],
            send_sem=part_send.at[i], recv_sem=part_recv.at[i],
            device_id=peer, device_id_type=MESH,
        )

    contract = (((1,), (1,)), ((), ()))

    def half_sum(i, chosen):
        return lax.dot_general(
            weight[span_of(i)], cols[chosen], contract, preferred_element_type=jnp.float32
        )

    @pl.loop(0, PARTS)
    def _(i):
        theirs[span_of(i)] = half_sum(i, other).astype(jnp.bfloat16)
        send_part(i).start()

    @pl.loop(0, PARTS)
    def _(i):
        ours[span_of(i)] = half_sum(i, own)

    for copy in hidden_copies:
        copy.wait()

    @pl.loop(0, cols.shape[1] // TILE)
    def _(i):
        span = pl.ds(pl.multiple_of(i * TILE, TILE), TILE)
        grad_weight[:, span] = jnp.dot(
            hidden[...], cols[own, span], preferred_element_type=jnp.float32
        ) + jnp.dot(other_hidden[...], cols[other, span], preferred_element_type=jnp.float32)

    store_weight = pltpu.make_async_copy(grad_weight, grad_weight_hbm, weight_sem)
    store_weight.start()

    def store(i):
        return pltpu.make_async_copy(
            grad_hidden.at[span_of(i)], grad_hidden_hbm.at[span_of(i)], store_sem.at[i]
        )

    @pl.loop(0, PARTS)
    def _(i):
        span = span_of(i)
        send_part(i).wait_recv()
        grad_hidden[span] = (ours[span] + arrived[span].astype(jnp.float32)).astype(jnp.bfloat16)
        store(i).start()

    @pl.loop(0, PARTS)
    def _(i):
        send_part(i).wait_send()
        store(i).wait()

    store_weight.wait()


def paired(acts, partner, hidden, down_weight):
    n_dp = lax.axis_size("dp")
    tokens, width = acts.shape
    rows, half = hidden.shape
    scale = float(tokens * n_dp * width * lax.axis_size("tensor"))
    rounds = n_dp.bit_length() - 1
    steps = n_dp // 4
    dma, bf16, f32 = pltpu.SemaphoreType.DMA, jnp.bfloat16, jnp.float32
    vmem, hbm = pl.BlockSpec(memory_space=pltpu.VMEM), pl.BlockSpec(memory_space=pltpu.HBM)
    grad_hidden, grad_weight, cka = pl.pallas_call(
        functools.partial(fused_kernel, n_dp, scale),
        out_shape=(
            jax.ShapeDtypeStruct((rows, half), bf16),
            jax.ShapeDtypeStruct((rows, width), f32),
            jax.ShapeDtypeStruct((8, 128), f32),
        ),
        in_specs=[hbm] * 4,
        out_specs=(hbm, hbm, vmem),
        scratch_shapes=[
            pltpu.VMEM((tokens, width), bf16), pltpu.VMEM((tokens, width), bf16),
            pltpu.VMEM((rows, half), bf16), pltpu.VMEM((rows, width), bf16),
            pltpu.VMEM((rows, half), bf16), pltpu.VMEM((n_dp * tokens, width), bf16),
            pltpu.VMEM((rows, half), bf16), pltpu.VMEM((rows, half), bf16),
            pltpu.VMEM((rows, half), f32), pltpu.VMEM((rows, half), bf16), pltpu.VMEM((rows, width), f32),
            pltpu.VMEM((2, 2, tokens, tokens), f32),
            pltpu.VMEM((2 * rounds + 1, 8, tokens), f32),
            dma((4,)), dma, dma((PARTS,)), dma((2,)), dma((2,)), dma, dma, dma((rounds,)), dma((rounds,)),
            dma((steps,)), dma((steps,)), dma((steps,)), dma((steps,)),
            dma((2 * steps,)), dma((2 * steps,)), dma((PARTS,)), dma((PARTS,)),
        ],
        compiler_params=pltpu.CompilerParams(
            collective_id=0, has_side_effects=True, vmem_limit_bytes=56 * 2**20
        ),
        cost_estimate=pl.CostEstimate(
            flops=8 * rows * half * width, transcendentals=0, bytes_accessed=16 * rows * width
        ),
    )(acts, partner, hidden, down_weight)
    return (grad_hidden, grad_weight, cka[0, 0])


def gathered(acts, partner, hidden, down_weight):
    rows = acts.shape[0]
    width = acts.shape[1] * lax.axis_size("tensor")
    total = rows * lax.axis_size("dp")
    scale = float(total * width)
    centered_x = center_rows(acts)
    centered_y = center_rows(partner)
    whole_x, whole_y = (
        lax.all_gather(centered_x, "tensor", axis=1, tiled=True),
        lax.all_gather(centered_y, "tensor", axis=1, tiled=True),
    )
    gram_x = token_gram(whole_x)
    gram_y = token_gram(whole_y)
    sxx, syy, sxy = lax.psum(
        (jnp.sum(gram_x * gram_x), jnp.sum(gram_y * gram_y), jnp.sum(gram_x * gram_y)), "dp"
    )
    root = jnp.sqrt(sxx * syy)
    cka = sxy / root
    ratio = sxy / sxx
    coef = -2.0 * scale / root
    mixed = gram_y - ratio * gram_x
    grad = (
        coef * jnp.dot(mixed, centered_x.astype(jnp.float32), precision=lax.Precision.HIGHEST)
    ).astype(jnp.bfloat16)
    columns = lax.all_gather(grad, "dp", axis=0, tiled=True)
    token_block = lax.all_to_all(columns, "tensor", split_axis=0, concat_axis=1, tiled=True)
    grad_hidden = lax.dot_general(
        lax.all_gather(down_weight, "tensor", axis=1, tiled=True),
        token_block,
        (((1,), (1,)), ((), ())),
        preferred_element_type=jnp.float32,
    ).astype(jnp.bfloat16)
    grad_weight = lax.dot_general(
        lax.all_gather(hidden, "tensor", axis=1, tiled=True),
        columns,
        (((1,), (0,)), ((), ())),
        preferred_element_type=jnp.float32,
    )
    return (grad_hidden, grad_weight, cka)


def solution(mesh):
    n_dp, n_tensor = mesh.shape["dp"], mesh.shape["tensor"]
    fits = n_tensor == 2 and n_dp >= 8 and n_dp & (n_dp - 1) == 0
    spec = P("dp", "tensor")
    return jax.shard_map(
        paired if fits else gathered,
        mesh=mesh, in_specs=(spec,) * 4, out_specs=(spec, spec, P()), check_vma=False,
    )
```

```python
import functools

import jax
import jax.numpy as jnp
from jax import lax
from jax.experimental import pallas as pl
from jax.experimental.pallas import tpu as pltpu
from jax.sharding import PartitionSpec as P

MESH = pl.DeviceIdType.MESH
FIRST = 64
PARTS = 7
TILE = 256


def center_rows(values):
    floats = values.astype(jnp.float32)
    return (floats - jnp.mean(floats, axis=0, keepdims=True)).astype(jnp.bfloat16)


def token_gram(values):
    return lax.dot_general(
        values, values, (((1,), (1,)), ((), ())), preferred_element_type=jnp.float32
    )


def fused_kernel(
    n_dp, scale, acts_hbm, partner_hbm, hidden_hbm, weight_hbm, grad_hidden_hbm, grad_weight_hbm, cka_ref,
    acts, partner, hidden, weight, other_hidden, cols, theirs, arrived, ours, grad_hidden, grad_weight, grams, stats,
    load_sem, weight_sem, store_sem, hid_send, hid_recv, gram_send, gram_recv, stat_send, stat_recv,
    up_send, up_recv, down_send, down_recv, sib_send, sib_recv, part_send, part_recv,
):
    tokens = acts.shape[0]
    rows = hidden.shape[0]
    chips, blocks_half = n_dp // 2, n_dp // 2
    side = chips // 2
    dp, tensor = lax.axis_index("dp"), lax.axis_index("tensor")
    chip, core = dp // 2, dp % 2
    column = chip % 2
    pos = (1 - column) * (chip // 2) + column * (chips - 1 - chip // 2)

    def chip_at(place):
        far = place // side
        return (1 - far) * (2 * place) + far * (2 * (chips - 1 - place) + 1)

    def device_at(offset):
        return chip_at((pos + offset + chips) % chips) * 2 + core

    def rows_of(block):
        half = (block // blocks_half + tensor) % 2
        return (half * blocks_half + block % blocks_half) * tokens

    loads = [
        pltpu.make_async_copy(source, target, load_sem.at[i])
        for i, (source, target) in enumerate(
            ((acts_hbm, acts), (partner_hbm, partner), (hidden_hbm, hidden), (weight_hbm, weight))
        )
    ]
    for load in loads:
        load.start()

    peer = (dp, 1 - tensor)
    sibling = (dp + 1 - 2 * core, tensor)
    above, below = (device_at(1), tensor), (device_at(-1), tensor)
    rounds = []
    bit = 1
    while bit < n_dp:
        rounds.append((dp + bit * (1 - 2 * ((dp // bit) % 2)), tensor))
        bit *= 2

    barrier = pltpu.get_barrier_semaphore()
    partners = [peer, above, below] + rounds
    for other in partners:
        pl.semaphore_signal(barrier, inc=1, device_id=other, device_id_type=MESH)
    pl.semaphore_wait(barrier, len(partners))

    def send_hidden(i, start, size):
        part = pl.ds(start, size)
        return pltpu.make_async_remote_copy(
            src_ref=hidden_hbm.at[part], dst_ref=other_hidden.at[part],
            send_sem=hid_send.at[i], recv_sem=hid_recv.at[i],
            device_id=peer, device_id_type=MESH,
        )

    hidden_copies = [send_hidden(0, 0, FIRST), send_hidden(1, FIRST, rows - FIRST)]
    hidden_copies[0].start()

    loads[0].wait()
    loads[1].wait()
    centered_x = center_rows(acts[...])
    centered_y = center_rows(partner[...])
    grams[0, 0] = token_gram(centered_x)
    grams[0, 1] = token_gram(centered_y)
    gram_copy = pltpu.make_async_remote_copy(
        src_ref=grams.at[0], dst_ref=grams.at[1], send_sem=gram_send, recv_sem=gram_recv,
        device_id=peer, device_id_type=MESH,
    )
    gram_copy.start()
    hidden_copies[1].start()
    gram_copy.wait()
    gram_x = grams[0, 0] + grams[1, 0]
    gram_y = grams[0, 1] + grams[1, 1]

    stats[0] = jnp.zeros_like(stats[0])
    stats[0, 0:1] = jnp.sum(gram_x * gram_x, axis=0, keepdims=True)
    stats[0, 1:2] = jnp.sum(gram_y * gram_y, axis=0, keepdims=True)
    stats[0, 2:3] = jnp.sum(gram_x * gram_y, axis=0, keepdims=True)
    for i, other in enumerate(rounds):
        copy = pltpu.make_async_remote_copy(
            src_ref=stats.at[2 * i], dst_ref=stats.at[2 * i + 1],
            send_sem=stat_send.at[i], recv_sem=stat_recv.at[i],
            device_id=other, device_id_type=MESH,
        )
        copy.start()
        copy.wait()
        stats[2 * i + 2] = stats[2 * i] + stats[2 * i + 1]
    sums = jnp.sum(stats[2 * len(rounds)], axis=1, keepdims=True)
    sxx, syy, sxy = sums[0:1], sums[1:2], sums[2:3]
    root = jnp.sqrt(sxx * syy)
    cka_ref[...] = sxy / root
    ratio = sxy / sxx
    coef = -2.0 * scale / root
    mixed = gram_y - ratio * gram_x
    grad = jnp.zeros(centered_x.shape, jnp.float32)
    rest = mixed
    for _ in range(3):
        top = rest.astype(jnp.bfloat16)
        rest = rest - top.astype(jnp.float32)
        grad += jnp.dot(top, centered_x, preferred_element_type=jnp.float32)
    own_rows = pl.ds(pl.multiple_of(rows_of(dp), tokens), tokens)
    cols[own_rows] = (coef * grad).astype(jnp.bfloat16)

    last = chips // 2

    def ring(step, way):
        block = device_at(-way * (step - 1))
        start, size = rows_of(block), tokens
        if step == last:
            size = tokens // 2
            start = start + (0 if way > 0 else size)
        span = pl.ds(pl.multiple_of(start, size), size)
        sends, recvs = (up_send, up_recv) if way > 0 else (down_send, down_recv)
        return pltpu.make_async_remote_copy(
            src_ref=cols.at[span], dst_ref=cols.at[span],
            send_sem=sends.at[step - 1], recv_sem=recvs.at[step - 1],
            device_id=above if way > 0 else below, device_id_type=MESH,
        )

    def share(i, block):
        span = pl.ds(pl.multiple_of(rows_of(block), tokens), tokens)
        return pltpu.make_async_remote_copy(
            src_ref=cols.at[span], dst_ref=cols.at[span],
            send_sem=sib_send.at[i], recv_sem=sib_recv.at[i],
            device_id=sibling, device_id_type=MESH,
        )

    ups = [ring(step, 1) for step in range(1, last + 1)]
    downs = [ring(step, -1) for step in range(1, last + 1)]
    ups[0].start()
    downs[0].start()
    shares = [share(0, dp)]
    shares[0].start()
    for step in range(1, last):
        for way, copies in ((1, ups), (-1, downs)):
            copies[step - 1].wait_recv()
            copies[step].start()
            shares.append(share(len(shares), device_at(-way * step)))
            shares[-1].start()
    ups[-1].wait_recv()
    downs[-1].wait_recv()
    shares.append(share(len(shares), device_at(last)))
    shares[-1].start()

    for copy in ups + downs:
        copy.wait_send()
    for copy in shares:
        copy.wait()
    loads[2].wait()
    loads[3].wait()

    half = n_dp * tokens // 2
    size = rows // PARTS
    own, other = pl.ds(0, half), pl.ds(half, half)

    def span_of(i):
        return pl.ds(pl.multiple_of(i * size, 16), size)

    def send_part(i):
        span = span_of(i)
        return pltpu.make_async_remote_copy(
            src_ref=theirs.at[span], dst_ref=arrived.at[span],
            send_sem=part_send.at[i], recv_sem=part_recv.at[i],
            device_id=peer, device_id_type=MESH,
        )

    contract = (((1,), (1,)), ((), ()))

    def half_sum(i, chosen):
        return lax.dot_general(
            weight[span_of(i)], cols[chosen], contract, preferred_element_type=jnp.float32
        )

    @pl.loop(0, PARTS)
    def _(i):
        theirs[span_of(i)] = half_sum(i, other).astype(jnp.bfloat16)
        send_part(i).start()

    @pl.loop(0, PARTS)
    def _(i):
        ours[span_of(i)] = half_sum(i, own)

    for copy in hidden_copies:
        copy.wait()

    @pl.loop(0, cols.shape[1] // TILE)
    def _(i):
        span = pl.ds(pl.multiple_of(i * TILE, TILE), TILE)
        grad_weight[:, span] = jnp.dot(
            hidden[...], cols[own, span], preferred_element_type=jnp.float32
        ) + jnp.dot(other_hidden[...], cols[other, span], preferred_element_type=jnp.float32)

    store_weight = pltpu.make_async_copy(grad_weight, grad_weight_hbm, weight_sem)
    store_weight.start()

    def store(i):
        return pltpu.make_async_copy(
            grad_hidden.at[span_of(i)], grad_hidden_hbm.at[span_of(i)], store_sem.at[i]
        )

    @pl.loop(0, PARTS)
    def _(i):
        span = span_of(i)
        send_part(i).wait_recv()
        grad_hidden[span] = (ours[span] + arrived[span].astype(jnp.float32)).astype(jnp.bfloat16)
        store(i).start()

    @pl.loop(0, PARTS)
    def _(i):
        send_part(i).wait_send()
        store(i).wait()

    store_weight.wait()


def paired(acts, partner, hidden, down_weight):
    n_dp = lax.axis_size("dp")
    tokens, width = acts.shape
    rows, half = hidden.shape
    scale = float(tokens * n_dp * width * lax.axis_size("tensor"))
    rounds = n_dp.bit_length() - 1
    steps = n_dp // 4
    dma, bf16, f32 = pltpu.SemaphoreType.DMA, jnp.bfloat16, jnp.float32
    vmem, hbm = pl.BlockSpec(memory_space=pltpu.VMEM), pl.BlockSpec(memory_space=pltpu.HBM)
    grad_hidden, grad_weight, cka = pl.pallas_call(
        functools.partial(fused_kernel, n_dp, scale),
        out_shape=(
            jax.ShapeDtypeStruct((rows, half), bf16),
            jax.ShapeDtypeStruct((rows, width), f32),
            jax.ShapeDtypeStruct((1, 1), f32),
        ),
        in_specs=[hbm] * 4,
        out_specs=(hbm, hbm, vmem),
        scratch_shapes=[
            pltpu.VMEM((tokens, width), bf16), pltpu.VMEM((tokens, width), bf16),
            pltpu.VMEM((rows, half), bf16), pltpu.VMEM((rows, width), bf16),
            pltpu.VMEM((rows, half), bf16), pltpu.VMEM((n_dp * tokens, width), bf16),
            pltpu.VMEM((rows, half), bf16), pltpu.VMEM((rows, half), bf16),
            pltpu.VMEM((rows, half), f32), pltpu.VMEM((rows, half), bf16), pltpu.VMEM((rows, width), f32),
            pltpu.VMEM((2, 2, tokens, tokens), f32),
            pltpu.VMEM((2 * rounds + 1, 8, tokens), f32),
            dma((4,)), dma, dma((PARTS,)), dma((2,)), dma((2,)), dma, dma, dma((rounds,)), dma((rounds,)),
            dma((steps,)), dma((steps,)), dma((steps,)), dma((steps,)),
            dma((2 * steps,)), dma((2 * steps,)), dma((PARTS,)), dma((PARTS,)),
        ],
        compiler_params=pltpu.CompilerParams(
            collective_id=0, has_side_effects=True, vmem_limit_bytes=56 * 2**20
        ),
        cost_estimate=pl.CostEstimate(
            flops=8 * rows * half * width, transcendentals=0, bytes_accessed=16 * rows * width
        ),
    )(acts, partner, hidden, down_weight)
    return (grad_hidden, grad_weight, cka.reshape(()))


def gathered(acts, partner, hidden, down_weight):
    rows = acts.shape[0]
    width = acts.shape[1] * lax.axis_size("tensor")
    total = rows * lax.axis_size("dp")
    scale = float(total * width)
    centered_x = center_rows(acts)
    centered_y = center_rows(partner)
    whole_x, whole_y = (
        lax.all_gather(centered_x, "tensor", axis=1, tiled=True),
        lax.all_gather(centered_y, "tensor", axis=1, tiled=True),
    )
    gram_x = token_gram(whole_x)
    gram_y = token_gram(whole_y)
    sxx, syy, sxy = lax.psum(
        (jnp.sum(gram_x * gram_x), jnp.sum(gram_y * gram_y), jnp.sum(gram_x * gram_y)), "dp"
    )
    root = jnp.sqrt(sxx * syy)
    cka = sxy / root
    ratio = sxy / sxx
    coef = -2.0 * scale / root
    mixed = gram_y - ratio * gram_x
    grad = (
        coef * jnp.dot(mixed, centered_x.astype(jnp.float32), precision=lax.Precision.HIGHEST)
    ).astype(jnp.bfloat16)
    columns = lax.all_gather(grad, "dp", axis=0, tiled=True)
    token_block = lax.all_to_all(columns, "tensor", split_axis=0, concat_axis=1, tiled=True)
    grad_hidden = lax.dot_general(
        lax.all_gather(down_weight, "tensor", axis=1, tiled=True),
        token_block,
        (((1,), (1,)), ((), ())),
        preferred_element_type=jnp.float32,
    ).astype(jnp.bfloat16)
    grad_weight = lax.dot_general(
        lax.all_gather(hidden, "tensor", axis=1, tiled=True),
        columns,
        (((1,), (0,)), ((), ())),
        preferred_element_type=jnp.float32,
    )
    return (grad_hidden, grad_weight, cka)


def solution(mesh):
    n_dp, n_tensor = mesh.shape["dp"], mesh.shape["tensor"]
    fits = n_tensor == 2 and n_dp >= 8 and n_dp & (n_dp - 1) == 0
    spec = P("dp", "tensor")
    return jax.shard_map(
        paired if fits else gathered,
        mesh=mesh, in_specs=(spec,) * 4, out_specs=(spec, spec, P()), check_vma=False,
    )
```
